512 devices in a mesh: prompt: 8 (over z_lo), sample: 16 (over x, z_hi, core), tensor: 4 (over y).
Axes of the slice: x: 4, y: 4, z: 16 (z_hi: 2, z_lo: 8; z = z_hi * 8 + z_lo), core: 2. Of those that a mesh axis runs over, the one named last changes fastest.
Arguments:
- queries: bfloat16 [128, 64, 4096], P(('prompt', 'sample'), None, 'tensor'), parts along dimension 0, may hold values from -15 to 15
- turn_kv: bfloat16 [2, 128, 64, 2048], P(None, ('prompt', 'sample'), None, 'tensor'), parts along dimension 1, may hold values from -6 to 6
- cache_kv: bfloat16 [2, 128, 448, 2048], P(None, ('prompt', 'sample'), None, 'tensor'), parts along dimension 1, may hold values from -6 to 6
- answer_len: int32 [128], P('prompt'), parts along dimension 0, may hold values from 1 to 448, 5376 in all
- out_weight: bfloat16 [4096, 4608], P('tensor', 'sample'), may hold values from -0.09375 to 0.09375
Outputs:
- mixed: bfloat16 [8192, 4608], P(('prompt', 'tensor'), 'sample'), parts along dimension 0
The draws below stay inside these ranges and needn't reach their ends.
There are 8 independent parts, one for each index of `prompt`. The reference program is written for one: setup_inputs(seed, part) draws one part's arguments, and reference() takes and returns one part's arrays. A program takes and returns all parts, laid end to end along the dimension named above; an argument that names none is the same for every part. Nothing has to cross between parts.
Inputs may be any that keep to these rules, and one draw needn't show every extreme that they name: `answer_len`: within each prompt, the lengths of its 16 agents sum to 5376, and some agent has all 448 slots live.
All inputs are finite; a program needn't handle non-finite values.
Results may differ from the reference program's by a relative error of at most 0.0057.
Values may be sent and summed in bfloat16 or wider, within the bound.
A program may use at most 128 MiB of HBM per device.

```python
import math
import jax
import jax.numpy as jnp
import numpy as np
from jax import lax

D = 4608
QH = 32
KVH = 16
HD = 128
TURN = 64
ANS_DEV = 448
AGENTS = 16


def shard_levels(rng, extent, cuts, least, largest):
    def one(axis_at, blocks):
        heights = jax.random.uniform(jax.random.fold_in(jax.random.fold_in(rng, 6), axis_at), (blocks,), jnp.float32, least / len(cuts), largest / len(cuts))
        return jnp.repeat(jnp.exp(heights), extent[axis_at] // blocks).reshape((-1,) + (1,) * (len(extent) - axis_at - 1))

    level = one(*cuts[0])
    for cut in cuts[1:]:
        level = level * one(*cut)
    return level


def split_up(count, total, reach, skew):
    portions = [(1 << 20) // math.isqrt(rank ** skew) + 1 for rank in range(2, count + 1)]
    spare, given = total - reach - (count - 1), [1] * (count - 1)
    while spare > 0:
        candidates = [i for i in range(count - 1) if given[i] < reach]
        whole, remaining = sum([portions[i] for i in candidates]), spare
        for i in candidates:
            more = min(reach - given[i], max(1, remaining * portions[i] // whole), spare)
            given[i] = given[i] + more
            spare = spare - more
    return np.array([reach] + given)


def uneven_parts(key, amount, total, most, skew):
    if amount == 2:
        one = jax.random.randint(key, (), max(1, total - most), min(most, total - 1) + 1)
        return jnp.stack([one, total - one])
    sizes = jnp.asarray(split_up(amount, total, most, skew), jnp.int32)
    twos = (amount - 1) // 2
    source_of, sink = sizes[1:1 + 2 * twos:2], sizes[2:2 + 2 * twos:2]
    slack = jnp.minimum(source_of - 1, most - sink)
    moved = jax.random.randint(jax.random.fold_in(key, 1), (twos,), 0, 1 << 20) % (slack + 1)
    sizes = sizes.at[1:1 + 2 * twos:2].set(source_of - moved).at[2:2 + 2 * twos:2].set(sink + moved)
    return sizes[jax.random.permutation(jax.random.fold_in(key, 2), amount)]


def gaussian(rng, dims, deviation, most, pieces=(), kind=jnp.bfloat16):
    level = shard_levels(rng, dims, pieces, -0.22, 0.18) if pieces else 1.0
    values = jax.random.normal(rng, dims, jnp.float32) * deviation * level
    return jnp.minimum(jnp.maximum(values, -most), most).astype(kind)


def setup_inputs(seed: int = 0, part: int = 0) -> dict:
    splits = jax.random.split(jax.random.key(seed), 6)
    part_keys = jax.random.split(jax.random.fold_in(splits[5], part), 6)
    return {
        "queries": gaussian(part_keys[0], (AGENTS, TURN, QH * HD), 2.5, 15.0, ((0, 16), (2, 4))),
        "turn_kv": gaussian(part_keys[1], (2, AGENTS, TURN, KVH * HD), 1.0, 6.0, ((1, 16), (3, 4))),
        "cache_kv": gaussian(part_keys[2], (2, AGENTS, ANS_DEV, KVH * HD), 1.0, 6.0, ((1, 16), (3, 4))),
        "answer_len": uneven_parts(part_keys[3], AGENTS, AGENTS * ANS_DEV * 3 // 4, ANS_DEV, 2).astype(jnp.int32),
        "out_weight": gaussian(splits[4], (QH * HD, D), (QH * HD) ** -0.5, 0.09375, ((0, 4), (1, 16))),
    }


softcap_value = 50.0
score_scale = 1.0 / 12.0


def attend_terms(query_rows, key_rows, value_rows, allowed):
    raw_scores = jnp.einsum("tkgd,skd->kgts", query_rows, key_rows) * score_scale
    capped = softcap_value * jnp.tanh(raw_scores / softcap_value)
    weights = jnp.exp(capped) * allowed
    totals = jnp.sum(weights, axis=-1)
    rounded = lax.optimization_barrier(weights.astype(jnp.bfloat16)).astype(jnp.float32)
    numerators = jnp.einsum("kgts,skd->tkgd", rounded, value_rows)
    return numerators, totals


def reference(queries, turn_kv, cache_kv, answer_len, out_weight):
    agent_count = queries.shape[0]
    group_size = QH // KVH
    all_keys = cache_kv[0].reshape(agent_count * ANS_DEV, KVH, HD).astype(jnp.float32)
    all_values = cache_kv[1].reshape(agent_count * ANS_DEV, KVH, HD).astype(jnp.float32)
    slot_ids = jnp.arange(agent_count * ANS_DEV, dtype=jnp.int32)
    owners = slot_ids // ANS_DEV
    valid = ((slot_ids % ANS_DEV) < answer_len[owners]).astype(jnp.float32)
    positions = jnp.arange(TURN, dtype=jnp.int32)
    causal = (positions[:, None] >= positions[None, :]).astype(jnp.float32)

    def one_agent(inputs):
        agent_queries, agent_keys, agent_values = inputs
        query_rows = agent_queries.reshape(TURN, KVH, group_size, HD).astype(jnp.float32)
        turn_keys = agent_keys.reshape(TURN, KVH, HD).astype(jnp.float32)
        turn_values = agent_values.reshape(TURN, KVH, HD).astype(jnp.float32)
        cache_num, cache_tot = attend_terms(query_rows, all_keys, all_values, valid)
        turn_num, turn_tot = attend_terms(query_rows, turn_keys, turn_values, causal)
        numerators = cache_num + turn_num
        totals = cache_tot + turn_tot
        attended = numerators / jnp.transpose(totals, (2, 0, 1))[..., None]
        return attended.reshape(TURN, QH * HD).astype(jnp.bfloat16)

    attended = lax.map(one_agent, (queries, turn_kv[0], turn_kv[1]))
    flat_rows = attended.reshape(agent_count * TURN, QH * HD)
    return jnp.dot(flat_rows, out_weight, preferred_element_type=jnp.float32).astype(jnp.bfloat16)
```

```python
import jax
import jax.numpy as jnp
from jax import lax
from jax.experimental import pallas as pl
from jax.experimental.pallas import tpu as pltpu
from jax.sharding import PartitionSpec as P

HD = 128
GROUP = 2
AGENTS = 16
TURN = 64
SLOTS = 448
HALF = 512
KHALF = 256
COLS = 288
NX = 4
NT = 4
STEP = 32
MESH = pl.DeviceIdType.MESH
F32 = jnp.float32
BF16 = jnp.bfloat16
NEAR, FAR = 0, 1

SCALE = 1.0 / 600.0
CAP_LOG2E = 50.0 * 1.4426950408889634


def weights_of(scores):
    return jnp.exp2(jnp.tanh(scores * SCALE) * CAP_LOG2E)


def dot_nt(a, b):
    return lax.dot_general(a, b, (((1,), (1,)), ((), ())), preferred_element_type=F32)


def kernel(
    len_ref, q_ref, turn_ref, cache_ref, w_ref, out_ref,
    q_all, kv, tkv, vext, tvext, w_all,
    pn, pt, xn, xt, own_n, own_t, zs, zn, zt, att, att_in, other, other_in,
    loc, qs_x, qr_x, qs_z, qr_z, qs_s, qr_s, fs, fr, ks, kr, ws, wr,
    ns, nr, ts, tr, zns, znr, zts, ztr, ats, atr, os_, or_,
):
    p, s, t = lax.axis_index("prompt"), lax.axis_index("sample"), lax.axis_index("tensor")
    x, h, c = lax.div(s, 4), lax.rem(lax.div(s, 2), 2), lax.rem(s, 2)
    o, g = 1 - c, 1 - h

    def at(xx, hh, cc, tt):
        return (p, xx * 4 + hh * 2 + cc, tt)

    def rem4(v):
        return lax.rem(v, 4)

    def remote(src, dst, send, recv, to):
        return pltpu.make_async_remote_copy(
            src_ref=src, dst_ref=dst, send_sem=send, recv_sem=recv, device_id=to, device_id_type=MESH
        )

    here = at(x, h, c, t)
    sibling = at(x, h, o, t)
    diagonal = t == x

    barrier = pltpu.get_barrier_semaphore()

    def greet(to):
        pl.semaphore_signal(barrier, inc=1, device_id=to, device_id_type=MESH)

    greet(sibling)
    for cc in range(2):
        greet(at(x, g, cc, t))
        for d in range(1, 4):
            greet(at(rem4(x + d), h, cc, t))
            greet(at(x, h, cc, rem4(t + d)))
    for d in range(1, 4):
        greet(at(t, h, c, rem4(t + d)))

    @pl.when(jnp.logical_not(diagonal))
    def _():
        greet(at(t, h, c, t))

    half = lambda cc: pl.ds(pl.multiple_of(cc * HALF, HALF), HALF)
    khalf = lambda cc: pl.ds(pl.multiple_of(cc * KHALF, KHALF), KHALF)
    mine = x * 4 + h * 2 + c
    local = [
        pltpu.make_async_copy(q_ref.at[0, :, half(c)], q_all.at[mine], loc.at[0]),
        pltpu.make_async_copy(cache_ref.at[:, 0, :, khalf(c)], kv.at[:, c], loc.at[1]),
        pltpu.make_async_copy(turn_ref.at[:, 0, :, khalf(c)], tkv.at[:, c], loc.at[2]),
        pltpu.make_async_copy(w_ref.at[half(c), :], w_all.at[t, c], loc.at[3]),
    ]
    for copy in local:
        copy.start()

    @pl.when(diagonal)
    def _():
        pl.semaphore_wait(barrier, 18)

    @pl.when(jnp.logical_not(diagonal))
    def _():
        pl.semaphore_wait(barrier, 19)

    def q_z(cc, tau):
        rows = pl.ds(tau * STEP, STEP)
        return remote(
            q_ref.at[0, rows, half(cc)], q_all.at[mine, rows], qs_z.at[cc, tau], qr_z.at[c, tau], at(x, g, cc, t)
        )

    def q_x(d, cc):
        return remote(
            q_ref.at[0, :, half(cc)], q_all.at[mine], qs_x.at[d - 1, cc], qr_x.at[d - 1, c], at(rem4(x + d), h, cc, t)
        )

    q_s = remote(q_ref.at[0, :, half(o)], q_all.at[mine], qs_s, qr_s, sibling)
    kv_s = [
        remote(cache_ref.at[:, 0, :, khalf(o)], kv.at[:, c], ks.at[0], kr.at[0], sibling),
        remote(turn_ref.at[:, 0, :, khalf(o)], tkv.at[:, c], ks.at[1], kr.at[1], sibling),
    ]
    sent = []

    def start(copy):
        copy.start()
        sent.append(copy)

    for tau in range(2):
        for cc in range(2):
            start(q_z(cc, tau))
    for d in (1, 3, 2):
        for cc in range(2):
            start(q_x(d, cc))
    start(q_s)
    for copy in kv_s:
        start(copy)

    def w_y(d, cc):
        return remote(
            w_ref.at[half(cc), :], w_all.at[t, c], ws.at[d, cc], wr.at[d, c], at(x, h, cc, rem4(t + d))
        )

    start(w_y(0, o))
    for d in (1, 3, 2):
        for cc in range(2):
            start(w_y(d, cc))

    for copy in local[1:3]:
        copy.wait()
    remote(kv.at[:, o], kv.at[:, o], ks.at[0], kr.at[0], sibling).wait_recv()
    remote(tkv.at[:, o], tkv.at[:, o], ks.at[1], kr.at[1], sibling).wait_recv()
    slot = lax.broadcasted_iota(jnp.int32, (SLOTS, HD), 0)
    for i in range(2):
        live = slot < len_ref[x * 4 + h * 2 + i]
        ones = jnp.where(live, 1.0, 0.0).astype(BF16)
        for k in range(2):
            value = kv[1, i, :, k * HD : (k + 1) * HD]
            vext[k, i, :, :HD] = jnp.where(live, value, jnp.zeros_like(value))
            vext[k, i, :, HD:] = ones
            tvext[k, i, :, :HD] = tkv[1, i, :, k * HD : (k + 1) * HD]
            tvext[k, i, :, HD:] = jnp.ones((TURN, HD), BF16)

    lane4 = lax.div(lax.broadcasted_iota(jnp.int32, (8, 128), 1), 4)

    def attend(nf, tau):
        hh = h if nf == NEAR else g
        rows = slice(tau * STEP, (tau + 1) * STEP)
        packed = [jnp.zeros((8, 128), F32) for _ in range(NX)]
        for k in range(2):
            pieces = []
            for d in range(NX):
                for cc in range(2):
                    a = rem4(x + d) * 4 + hh * 2 + cc
                    for gg in range(GROUP):
                        col = (k * GROUP + gg) * HD
                        pieces.append(q_all[a, rows, col : col + HD])
            q = jnp.concatenate(pieces, axis=0)
            acc = jnp.zeros((q.shape[0], 2 * HD), F32)
            for i in range(2):
                key = kv[0, i, :, k * HD : (k + 1) * HD]
                w = weights_of(dot_nt(q, key)).astype(BF16)
                acc = acc + jnp.dot(w, vext[k, i], preferred_element_type=F32)
            blocks = []
            for d in range(NX):
                for cc in range(2):
                    lo = (d * 2 + cc) * GROUP * STEP
                    block = acc[lo : lo + GROUP * STEP]
                    if nf == NEAR and d == 0:
                        key = tkv[0, cc, :, k * HD : (k + 1) * HD]
                        w = weights_of(dot_nt(q[lo : lo + GROUP * STEP], key))
                        shape = (GROUP * STEP, TURN)
                        token = lax.rem(lax.broadcasted_iota(jnp.int32, shape, 0), STEP) + tau * STEP
                        u = lax.broadcasted_iota(jnp.int32, shape, 1)
                        w = jnp.where(u <= token, w, 0.0).astype(BF16)
                        block = block + jnp.dot(w, tvext[k, cc], preferred_element_type=F32)
                    for gg in range(GROUP):
                        col = (k * GROUP + gg) * HD
                        part = block[gg * STEP : (gg + 1) * STEP]
                        to = slice(cc * STEP, (cc + 1) * STEP)
                        if d == 0:
                            own_n[nf, tau, to, col : col + HD] = part[:, :HD]
                        else:
                            pn[nf, tau, d - 1, to, col : col + HD] = part[:, :HD].astype(BF16)
                        for i in range(STEP // 8):
                            index = 4 * (cc * (STEP // 8) + i) + k * GROUP + gg
                            packed[d] = jnp.where(lane4 == index, part[i * 8 : (i + 1) * 8, HD:], packed[d])
        own_t[nf, tau] = packed[0]
        for d in range(1, NX):
            pt[nf, tau, d - 1] = packed[d]

    def x_n(nf, tau, d):
        j = d - 1
        return remote(
            pn.at[nf, tau, j], xn.at[nf, tau, j], ns.at[nf, tau, j], nr.at[nf, tau, j], at(rem4(x + d), h, c, t)
        )

    def x_t(nf, tau, d):
        j = d - 1
        return remote(
            pt.at[nf, tau, j], xt.at[nf, tau, j], ts.at[nf, tau, j], tr.at[nf, tau, j], at(rem4(x + d), h, c, t)
        )

    def spread(nf, tau):
        for d in (2, 1, 3):
            start(x_n(nf, tau, d))
            start(x_t(nf, tau, d))

    def z_n(nf, tau):
        return remote(
            zs.at[nf, tau], zn.at[1 - nf, tau], zns.at[nf, tau], znr.at[1 - nf, tau], at(x, g, c, t)
        )

    def z_t(nf, tau):
        return remote(
            own_t.at[nf, tau], zt.at[1 - nf, tau], zts.at[nf, tau], ztr.at[1 - nf, tau], at(x, g, c, t)
        )

    def reduce(nf, tau):
        for d in range(1, NX):
            x_n(nf, tau, d).wait_recv()
            x_t(nf, tau, d).wait_recv()
        total = own_n[nf, tau]
        tiny = own_t[nf, tau]
        for j in range(NX - 1):
            total = total + xn[nf, tau, j].astype(F32)
            tiny = tiny + xt[nf, tau, j]
        own_n[nf, tau] = total
        own_t[nf, tau] = tiny
        zs[nf, tau] = total.astype(BF16)
        start(z_n(nf, tau))
        start(z_t(nf, tau))

    def a_to(nf, tau, d):
        return remote(
            att.at[nf, tau], att_in.at[nf, tau, t], ats.at[nf, tau, d], atr.at[nf, tau, t], at(rem4(x + d), h, c, x)
        )

    def a_self(nf, tau):
        return pltpu.make_async_copy(att.at[nf, tau], att_in.at[nf, tau, t], atr.at[nf, tau, t])

    def combine(nf, tau):
        z_n(1 - nf, tau).wait_recv()
        z_t(1 - nf, tau).wait_recv()
        tiny = own_t[nf, tau] + zt[nf, tau]
        for hd in range(2 * GROUP):
            cols = slice(hd * HD, (hd + 1) * HD)
            total = jnp.concatenate(
                [
                    jnp.broadcast_to(tiny[:, 4 * (4 * i + hd) : 4 * (4 * i + hd) + 1], (8, HD))
                    for i in range(2 * STEP // 8)
                ],
                axis=0,
            )
            numer = own_n[nf, tau, :, cols] + zn[nf, tau, :, cols].astype(F32)
            att[nf, tau, :, cols] = (numer / total).astype(BF16)
        for d in (2, 1, 3):
            start(a_to(nf, tau, d))

        @pl.when(diagonal)
        def _():
            a_self(nf, tau).start()

        @pl.when(jnp.logical_not(diagonal))
        def _():
            a_to(nf, tau, 0).start()

    def o_s(nf, tau):
        return remote(other.at[nf, tau], other_in.at[nf, tau], os_.at[nf, tau], or_.at[nf, tau], sibling)

    held = {}

    def project(nf, taus):
        for tau in taus:
            for j in range(NT):
                remote(
                    att.at[nf, tau], att_in.at[nf, tau, j], ats.at[nf, tau, 1], atr.at[nf, tau, j], sibling
                ).wait_recv()
        rows = len(taus) * 2 * STEP
        for which in (o, c):
            acc = jnp.zeros((rows, COLS), F32)
            for j in range(NT):
                a = jnp.concatenate([att_in[nf, tau, j] for tau in taus], axis=0)
                acc = acc + jnp.dot(a, w_all[j, which], preferred_element_type=F32)
            if which is o:
                for n, tau in enumerate(taus):
                    other[nf, tau] = acc[n * 2 * STEP : (n + 1) * 2 * STEP]
                    start(o_s(nf, tau))
            else:
                for n, tau in enumerate(taus):
                    held[nf, tau] = acc[n * 2 * STEP : (n + 1) * 2 * STEP]

    def finish(nf, tau):
        o_s(nf, tau).wait_recv()
        hh = h if nf == NEAR else g
        block = (held[nf, tau] + other_in[nf, tau]).astype(BF16)
        for cc in range(2):
            row = pl.multiple_of((hh * 2 + cc) * TURN + tau * STEP, STEP)
            out_ref[pl.ds(row, STEP), :] = block[cc * STEP : (cc + 1) * STEP]

    def q_f(tau, d):
        pair = q_all.at[pl.ds(x * 4 + g * 2, 2), pl.ds(tau * STEP, STEP)]
        return remote(pair, pair, fs.at[d - 1, tau], fr.at[d - 1, tau], at(rem4(x + d), h, c, t))

    def forward(tau):
        rows = pl.ds(tau * STEP, STEP)
        for cc in range(2):
            into = q_all.at[x * 4 + g * 2 + cc, rows]
            remote(into, into, qs_z.at[cc, tau], qr_z.at[cc, tau], at(x, g, cc, t)).wait_recv()
        for d in (2, 1, 3):
            start(q_f(tau, d))

    def forwarded(tau):
        for d in range(1, NX):
            pair = q_all.at[pl.ds(rem4(x - d + 4) * 4 + g * 2, 2), pl.ds(tau * STEP, STEP)]
            remote(pair, pair, fs.at[d - 1, tau], fr.at[d - 1, tau], sibling).wait_recv()

    local[0].wait()
    into = q_all.at[x * 4 + h * 2 + o]
    remote(into, into, qs_s, qr_s, sibling).wait_recv()
    for d in range(1, NX):
        for cc in range(2):
            into = q_all.at[rem4(x - d + 4) * 4 + h * 2 + cc]
            remote(into, into, qs_x.at[d - 1, cc], qr_x.at[d - 1, cc], sibling).wait_recv()

    attend(NEAR, 0)
    spread(NEAR, 0)
    attend(NEAR, 1)
    spread(NEAR, 1)
    forward(0)
    reduce(NEAR, 0)
    reduce(NEAR, 1)
    forward(1)
    forwarded(0)
    attend(FAR, 0)
    spread(FAR, 0)
    forwarded(1)
    attend(FAR, 1)
    spread(FAR, 1)
    reduce(FAR, 0)
    combine(FAR, 0)
    reduce(FAR, 1)
    combine(FAR, 1)
    local[3].wait()
    for d in range(NT):
        for cc in range(2):
            if d:
                into = w_all.at[rem4(t - d + 4), cc]
                remote(into, into, ws.at[d, cc], wr.at[d, cc], sibling).wait_recv()
    into = w_all.at[t, o]
    remote(into, into, ws.at[0, o], wr.at[0, o], sibling).wait_recv()
    project(FAR, (0, 1))
    finish(FAR, 0)
    finish(FAR, 1)
    combine(NEAR, 0)
    project(NEAR, (0,))
    combine(NEAR, 1)
    finish(NEAR, 0)
    project(NEAR, (1,))
    finish(NEAR, 1)

    for copy in sent:
        copy.wait_send()

    @pl.when(jnp.logical_not(diagonal))
    def _():
        for nf in range(2):
            for tau in range(2):
                a_to(nf, tau, 0).wait_send()


def on_device(queries, turn_kv, cache_kv, answer_len, out_weight):
    dma = lambda *shape: pltpu.SemaphoreType.DMA(shape)
    any_space = pl.BlockSpec(memory_space=pl.ANY)
    rows = 2 * STEP
    return pl.pallas_call(
        kernel,
        out_shape=jax.ShapeDtypeStruct((4 * TURN, COLS), BF16),
        in_specs=[pl.BlockSpec(memory_space=pltpu.SMEM)] + [any_space] * 4,
        out_specs=pl.BlockSpec(memory_space=pltpu.VMEM),
        scratch_shapes=[
            pltpu.VMEM((AGENTS, TURN, HALF), BF16),
            pltpu.VMEM((2, 2, SLOTS, KHALF), BF16),
            pltpu.VMEM((2, 2, TURN, KHALF), BF16),
            pltpu.VMEM((2, 2, SLOTS, 2 * HD), BF16),
            pltpu.VMEM((2, 2, TURN, 2 * HD), BF16),
            pltpu.VMEM((NT, 2, HALF, COLS), BF16),
            pltpu.VMEM((2, 2, NX - 1, rows, HALF), BF16),
            pltpu.VMEM((2, 2, NX - 1, 8, 128), F32),
            pltpu.VMEM((2, 2, NX - 1, rows, HALF), BF16),
            pltpu.VMEM((2, 2, NX - 1, 8, 128), F32),
            pltpu.VMEM((2, 2, rows, HALF), F32),
            pltpu.VMEM((2, 2, 8, 128), F32),
            pltpu.VMEM((2, 2, rows, HALF), BF16),
            pltpu.VMEM((2, 2, rows, HALF), BF16),
            pltpu.VMEM((2, 2, 8, 128), F32),
            pltpu.VMEM((2, 2, rows, HALF), BF16),
            pltpu.VMEM((2, 2, NT, rows, HALF), BF16),
            pltpu.VMEM((2, 2, rows, COLS), F32),
            pltpu.VMEM((2, 2, rows, COLS), F32),
            dma(4),
            dma(3, 2), dma(3, 2),
            dma(2, 2), dma(2, 2),
            pltpu.SemaphoreType.DMA, pltpu.SemaphoreType.DMA,
            dma(3, 2), dma(3, 2),
            dma(2), dma(2),
            dma(NT, 2), dma(NT, 2),
            dma(2, 2, 3), dma(2, 2, 3),
            dma(2, 2, 3), dma(2, 2, 3),
            dma(2, 2), dma(2, 2),
            dma(2, 2), dma(2, 2),
            dma(2, 2, 4), dma(2, 2, 4),
            dma(2, 2), dma(2, 2),
        ],
        compiler_params=pltpu.CompilerParams(
            collective_id=0, has_side_effects=True, vmem_limit_bytes=48 * 2**20
        ),
    )(answer_len, queries, turn_kv, cache_kv, out_weight)


def solution(mesh):
    return jax.shard_map(
        on_device,
        mesh=mesh,
        in_specs=(
            P(("prompt", "sample"), None, "tensor"),
            P(None, ("prompt", "sample"), None, "tensor"),
            P(None, ("prompt", "sample"), None, "tensor"),
            P("prompt"),
            P("tensor", "sample"),
        ),
        out_specs=P(("prompt", "tensor"), "sample"),
        check_vma=False,
    )
```

```python
import jax
import jax.numpy as jnp
from jax import lax
from jax.experimental import pallas as pl
from jax.experimental.pallas import tpu as pltpu
from jax.sharding import PartitionSpec as P

HD = 128
GROUP = 2
AGENTS = 16
TURN = 64
SLOTS = 448
HALF = 512
KHALF = 256
COLS = 288
NX = 4
NT = 4
CHUNKS = 4
STEP = TURN // CHUNKS
TALLY = (2 * STEP * HALF * 2 + 8 * 128 * 4) // 512
MESH = pl.DeviceIdType.MESH
F32 = jnp.float32
BF16 = jnp.bfloat16
NEAR, FAR = 0, 1

SCALE = 1.0 / 600.0
CAP_LOG2E = 50.0 * 1.4426950408889634


def weights_of(scores):
    return jnp.exp2(jnp.tanh(scores * SCALE) * CAP_LOG2E)


def dot_nt(a, b):
    return lax.dot_general(a, b, (((1,), (1,)), ((), ())), preferred_element_type=F32)


def kernel(
    len_ref, q_ref, turn_ref, cache_ref, w_ref, out_ref,
    q_all, kv, tkv, vext, tvext, w_all,
    pn, pt, xn, xt, own_n, own_t, zs, zn, zt, att, att_in, other, other_in,
    tally, loc, qs, qr_x, qr_z, qr_s, fr, ks, kr, ws, wr,
    ns, ts, xr, zns, zts, zr, ats, atr, os_, or_,
):
    p, s, t = lax.axis_index("prompt"), lax.axis_index("sample"), lax.axis_index("tensor")
    x, h, c = lax.div(s, 4), lax.rem(lax.div(s, 2), 2), lax.rem(s, 2)
    o, g = 1 - c, 1 - h

    def at(xx, hh, cc, tt):
        return (p, xx * 4 + hh * 2 + cc, tt)

    def rem4(v):
        return lax.rem(v, 4)

    def remote(src, dst, send, recv, to):
        return pltpu.make_async_remote_copy(
            src_ref=src, dst_ref=dst, send_sem=send, recv_sem=recv, device_id=to, device_id_type=MESH
        )

    here = at(x, h, c, t)
    sibling = at(x, h, o, t)
    diagonal = t == x

    barrier = pltpu.get_barrier_semaphore()

    def greet(to):
        pl.semaphore_signal(barrier, inc=1, device_id=to, device_id_type=MESH)

    for cc in range(2):
        greet(at(x, g, cc, t))
    greet(sibling)
    for cc in range(2):
        for d in range(1, 4):
            greet(at(rem4(x + d), h, cc, t))
            greet(at(x, h, cc, rem4(t + d)))
    for d in range(1, 4):
        greet(at(t, h, c, rem4(t + d)))

    @pl.when(jnp.logical_not(diagonal))
    def _():
        greet(at(t, h, c, t))

    half = lambda cc: pl.ds(pl.multiple_of(cc * HALF, HALF), HALF)
    khalf = lambda cc: pl.ds(pl.multiple_of(cc * KHALF, KHALF), KHALF)
    mine = x * 4 + h * 2 + c
    local = [
        pltpu.make_async_copy(q_ref.at[0, :, half(c)], q_all.at[mine], loc.at[0]),
        pltpu.make_async_copy(cache_ref.at[:, 0, :, khalf(c)], kv.at[:, c], loc.at[1]),
        pltpu.make_async_copy(turn_ref.at[:, 0, :, khalf(c)], tkv.at[:, c], loc.at[2]),
        pltpu.make_async_copy(w_ref.at[:, half(c)], w_all.at[t * 2 + c], loc.at[3]),
    ]
    for copy in local:
        copy.start()

    @pl.when(diagonal)
    def _():
        pl.semaphore_wait(barrier, 18)

    @pl.when(jnp.logical_not(diagonal))
    def _():
        pl.semaphore_wait(barrier, 19)

    def q_z(cc, tau):
        rows = pl.ds(tau * STEP, STEP)
        return remote(
            q_ref.at[0, rows, half(cc)], q_all.at[mine, rows], qs, qr_z.at[tau], at(x, g, cc, t)
        )

    def q_x(d, cc, tau):
        rows = pl.ds(tau * STEP, STEP)
        return remote(
            q_ref.at[0, rows, half(cc)], q_all.at[mine, rows],
            qs, qr_x.at[tau], at(rem4(x + d), h, cc, t),
        )

    q_s = remote(q_ref.at[0, :, half(o)], q_all.at[mine], qs, qr_s, sibling)
    kv_s = [
        remote(cache_ref.at[:, 0, :, khalf(o)], kv.at[:, c], ks, kr, sibling),
        remote(turn_ref.at[:, 0, :, khalf(o)], tkv.at[:, c], ks, kr, sibling),
    ]

    def start(copy):
        copy.start()

    def arrived(ref, semaphore):
        pltpu.make_async_copy(ref, ref, semaphore).wait()

    def queries_out(tau):
        for d in (1, 3, 2):
            for cc in range(2):
                start(q_x(d, cc, tau))

    def queries_over(tau):
        for cc in range(2):
            start(q_z(cc, tau))

    def keys_out():
        start(q_s)
        for copy in kv_s:
            start(copy)

    def w_y(d, cc):
        return remote(
            w_ref.at[:, half(cc)], w_all.at[t * 2 + c], ws, wr, at(x, h, cc, rem4(t + d))
        )

    def weights_out():
        start(w_y(0, o))
        for d in (1, 3, 2):
            for cc in range(2):
                start(w_y(d, cc))

    def values_in():
        for copy in local[1:3]:
            copy.wait()
        arrived(q_all.at[pl.ds(0, 8)], kr)
        slot = lax.broadcasted_iota(jnp.int32, (SLOTS, HD), 0)
        for i in range(2):
            live = slot < len_ref[x * 4 + h * 2 + i]
            ones = jnp.where(live, 1.0, 0.0).astype(BF16)
            for k in range(2):
                value = kv[1, i, :, k * HD : (k + 1) * HD]
                vext[k, i, :, :HD] = jnp.where(live, value, jnp.zeros_like(value))
                vext[k, i, :, HD:] = ones
                tvext[k, i, :, :HD] = tkv[1, i, :, k * HD : (k + 1) * HD]
                tvext[k, i, :, HD:] = jnp.ones((TURN, HD), BF16)

    lane4 = lax.div(lax.broadcasted_iota(jnp.int32, (8, 128), 1), 4)

    def attend(nf, tau):
        hh = h if nf == NEAR else g
        rows = slice(tau * STEP, (tau + 1) * STEP)
        packed = [jnp.zeros((8, 128), F32) for _ in range(NX)]
        for k in range(2):
            pieces = []
            for d in range(NX):
                for cc in range(2):
                    a = rem4(x + d) * 4 + hh * 2 + cc
                    for gg in range(GROUP):
                        col = (k * GROUP + gg) * HD
                        pieces.append(q_all[a, rows, col : col + HD])
            q = jnp.concatenate(pieces, axis=0)
            acc = jnp.zeros((q.shape[0], 2 * HD), F32)
            for i in range(2):
                key = kv[0, i, :, k * HD : (k + 1) * HD]
                w = weights_of(dot_nt(q, key)).astype(BF16)
                acc = acc + jnp.dot(w, vext[k, i], preferred_element_type=F32)
            blocks = []
            for d in range(NX):
                for cc in range(2):
                    lo = (d * 2 + cc) * GROUP * STEP
                    block = acc[lo : lo + GROUP * STEP]
                    if nf == NEAR and d == 0:
                        key = tkv[0, cc, :, k * HD : (k + 1) * HD]
                        w = weights_of(dot_nt(q[lo : lo + GROUP * STEP], key))
                        shape = (GROUP * STEP, TURN)
                        token = lax.rem(lax.broadcasted_iota(jnp.int32, shape, 0), STEP) + tau * STEP
                        u = lax.broadcasted_iota(jnp.int32, shape, 1)
                        w = jnp.where(u <= token, w, 0.0).astype(BF16)
                        block = block + jnp.dot(w, tvext[k, cc], preferred_element_type=F32)
                    for gg in range(GROUP):
                        col = (k * GROUP + gg) * HD
                        part = block[gg * STEP : (gg + 1) * STEP]
                        to = slice(cc * STEP, (cc + 1) * STEP)
                        if d == 0:
                            own_n[nf, tau, to, col : col + HD] = part[:, :HD]
                        else:
                            pn[nf, tau, d - 1, to, col : col + HD] = part[:, :HD].astype(BF16)
                        for i in range(STEP // 8):
                            index = 4 * (cc * (STEP // 8) + i) + k * GROUP + gg
                            packed[d] = jnp.where(lane4 == index, part[i * 8 : (i + 1) * 8, HD:], packed[d])
        own_t[nf, tau] = packed[0]
        for d in range(1, NX):
            pt[nf, tau, d - 1] = packed[d]

    def x_n(nf, tau, d):
        j = d - 1
        return remote(
            pn.at[nf, tau, j], xn.at[nf, tau, j], ns, xr.at[nf, tau], at(rem4(x + d), h, c, t)
        )

    def x_t(nf, tau, d):
        j = d - 1
        return remote(
            pt.at[nf, tau, j], xt.at[nf, tau, j], ts, xr.at[nf, tau], at(rem4(x + d), h, c, t)
        )

    def spread(nf, tau):
        for d in (2, 1, 3):
            start(x_n(nf, tau, d))
            start(x_t(nf, tau, d))

    def z_n(nf, tau):
        return remote(
            zs.at[nf, tau], zn.at[1 - nf, tau], zns, zr.at[1 - nf, tau], at(x, g, c, t)
        )

    def z_t(nf, tau):
        return remote(
            own_t.at[nf, tau], zt.at[1 - nf, tau], zts, zr.at[1 - nf, tau], at(x, g, c, t)
        )

    def reduce(nf, tau):
        arrived(tally, xr.at[nf, tau])
        total = own_n[nf, tau]
        tiny = own_t[nf, tau]
        for j in range(NX - 1):
            total = total + xn[nf, tau, j].astype(F32)
            tiny = tiny + xt[nf, tau, j]
        own_n[nf, tau] = total
        own_t[nf, tau] = tiny
        zs[nf, tau] = total.astype(BF16)
        start(z_n(nf, tau))
        start(z_t(nf, tau))

    def a_to(nf, tau, d):
        return remote(
            att.at[nf, tau], att_in.at[nf, tau, t], ats, atr.at[nf, tau], at(rem4(x + d), h, c, x)
        )

    def a_self(nf, tau):
        return pltpu.make_async_copy(att.at[nf, tau], att_in.at[nf, tau, t], atr.at[nf, tau])

    def combine(nf, tau):
        arrived(tally.at[pl.ds(0, TALLY)], zr.at[nf, tau])
        tiny = own_t[nf, tau] + zt[nf, tau]
        for hd in range(2 * GROUP):
            cols = slice(hd * HD, (hd + 1) * HD)
            total = jnp.concatenate(
                [
                    jnp.broadcast_to(tiny[:, 4 * (4 * i + hd) : 4 * (4 * i + hd) + 1], (8, HD))
                    for i in range(2 * STEP // 8)
                ],
                axis=0,
            )
            numer = own_n[nf, tau, :, cols] + zn[nf, tau, :, cols].astype(F32)
            att[nf, tau, :, cols] = (numer / total).astype(BF16)
        for d in (2, 1, 3):
            start(a_to(nf, tau, d))

        @pl.when(diagonal)
        def _():
            a_self(nf, tau).start()

        @pl.when(jnp.logical_not(diagonal))
        def _():
            a_to(nf, tau, 0).start()

    def o_s(group, nf, taus):
        these = other.at[nf, pl.ds(taus[0], len(taus))]
        into = other_in.at[nf, pl.ds(taus[0], len(taus))]
        return remote(these, into, os_, or_.at[group], sibling)

    held = {}

    def att_arrived(nf, tau):
        arrived(att_in.at[nf, tau], atr.at[nf, tau])

    def project(group, nf, taus):
        for which in (o, c):
            acc = jnp.zeros((len(taus) * 2 * STEP, COLS), F32)
            for j in range(NT):
                a = jnp.concatenate([att_in[nf, tau, j] for tau in taus], axis=0)
                acc = acc + dot_nt(a, w_all[j * 2 + which])
            for n, tau in enumerate(taus):
                part = acc[n * 2 * STEP : (n + 1) * 2 * STEP]
                if which is o:
                    other[nf, tau] = part
                else:
                    held[nf, tau] = part
            if which is o:
                start(o_s(group, nf, taus))

    def finish(group, nf, taus):
        arrived(other_in.at[nf, pl.ds(taus[0], len(taus))], or_.at[group])
        hh = h if nf == NEAR else g
        for tau in taus:
            block = (held[nf, tau] + other_in[nf, tau]).astype(BF16)
            for cc in range(2):
                row = pl.multiple_of((hh * 2 + cc) * TURN + tau * STEP, STEP)
                out_ref[pl.ds(row, STEP), :] = block[cc * STEP : (cc + 1) * STEP]

    def q_f(tau, d):
        pair = q_all.at[pl.ds(x * 4 + g * 2, 2), pl.ds(tau * STEP, STEP)]
        return remote(pair, pair, qs, fr.at[tau], at(rem4(x + d), h, c, t))

    def forward(tau):
        arrived(q_all.at[pl.ds(0, 2), pl.ds(0, STEP)], qr_z.at[tau])
        for d in (2, 1, 3):
            start(q_f(tau, d))

    def forwarded(tau):
        arrived(q_all.at[pl.ds(0, 6), pl.ds(0, STEP)], fr.at[tau])

    def near_in(tau):
        arrived(q_all.at[pl.ds(0, 6), pl.ds(0, STEP)], qr_x.at[tau])

    def own_in():
        local[0].wait()
        arrived(q_all.at[0], qr_s)

    def weights_in():
        local[3].wait()
        arrived(w_all.at[pl.ds(0, 7)], wr)

    def leave():
        arrived(q_all.at[pl.ds(0, 15)], qs)
        arrived(q_all.at[pl.ds(0, 8)], ks)
        arrived(w_all.at[pl.ds(0, 7)], ws)
        arrived(pn, ns)
        arrived(pt, ts)
        arrived(zs, zns)
        arrived(own_t, zts)

    queries_over(0)
    queries_out(0)
    keys_out()
    weights_out()
    values_in()
    queries_over(1)
    queries_out(1)
    own_in()
    near_in(0)
    queries_over(2)
    queries_out(2)
    attend(NEAR, 0)
    spread(NEAR, 0)
    near_in(1)
    queries_over(3)
    queries_out(3)
    attend(NEAR, 1)
    spread(NEAR, 1)
    forward(0)
    near_in(2)
    attend(NEAR, 2)
    spread(NEAR, 2)
    reduce(NEAR, 0)
    forward(1)
    near_in(3)
    attend(NEAR, 3)
    spread(NEAR, 3)
    reduce(NEAR, 1)
    forwarded(0)
    attend(FAR, 0)
    forward(2)
    spread(FAR, 0)
    reduce(NEAR, 2)
    forwarded(1)
    attend(FAR, 1)
    forward(3)
    spread(FAR, 1)
    reduce(NEAR, 3)
    forwarded(2)
    attend(FAR, 2)
    spread(FAR, 2)
    reduce(FAR, 0)
    forwarded(3)
    attend(FAR, 3)
    spread(FAR, 3)
    combine(FAR, 0)
    reduce(FAR, 1)
    combine(FAR, 1)
    reduce(FAR, 2)
    combine(FAR, 2)
    reduce(FAR, 3)
    combine(FAR, 3)
    weights_in()
    combine(NEAR, 0)
    combine(NEAR, 1)
    combine(NEAR, 2)
    att_arrived(FAR, 0)
    att_arrived(FAR, 1)
    att_arrived(FAR, 2)
    att_arrived(FAR, 3)
    project(0, FAR, (0, 1, 2, 3))
    combine(NEAR, 3)
    att_arrived(NEAR, 0)
    att_arrived(NEAR, 1)
    att_arrived(NEAR, 2)
    project(1, NEAR, (0, 1, 2))
    finish(0, FAR, (0, 1, 2, 3))
    finish(1, NEAR, (0, 1, 2))
    att_arrived(NEAR, 3)
    project(2, NEAR, (3,))
    leave()
    finish(2, NEAR, (3,))

    arrived(other, os_)

    @pl.when(diagonal)
    def _():
        arrived(att_in.at[:, :, pl.ds(0, 3)], ats)

    @pl.when(jnp.logical_not(diagonal))
    def _():
        arrived(att_in, ats)


def on_device(queries, turn_kv, cache_kv, answer_len, out_weight):
    dma = lambda *shape: pltpu.SemaphoreType.DMA(shape)
    far_memory = lambda array: pltpu.with_memory_space_constraint(array, pltpu.HBM)
    hbm = pl.BlockSpec(memory_space=pltpu.HBM)
    one = pltpu.SemaphoreType.DMA
    rows = 2 * STEP
    return pl.pallas_call(
        kernel,
        out_shape=pltpu.VMEM((4 * TURN, COLS), BF16),
        in_specs=[pl.BlockSpec(memory_space=pltpu.SMEM)] + [hbm] * 4,
        out_specs=pl.BlockSpec(memory_space=pltpu.VMEM),
        scratch_shapes=[
            pltpu.VMEM((AGENTS, TURN, HALF), BF16),
            pltpu.VMEM((2, 2, SLOTS, KHALF), BF16),
            pltpu.VMEM((2, 2, TURN, KHALF), BF16),
            pltpu.VMEM((2, 2, SLOTS, 2 * HD), BF16),
            pltpu.VMEM((2, 2, TURN, 2 * HD), BF16),
            pltpu.VMEM((NT * 2, COLS, HALF), BF16),
            pltpu.VMEM((2, CHUNKS, NX - 1, rows, HALF), BF16),
            pltpu.VMEM((2, CHUNKS, NX - 1, 8, 128), F32),
            pltpu.VMEM((2, CHUNKS, NX - 1, rows, HALF), BF16),
            pltpu.VMEM((2, CHUNKS, NX - 1, 8, 128), F32),
            pltpu.VMEM((2, CHUNKS, rows, HALF), F32),
            pltpu.VMEM((2, CHUNKS, 8, 128), F32),
            pltpu.VMEM((2, CHUNKS, rows, HALF), BF16),
            pltpu.VMEM((2, CHUNKS, rows, HALF), BF16),
            pltpu.VMEM((2, CHUNKS, 8, 128), F32),
            pltpu.VMEM((2, CHUNKS, rows, HALF), BF16),
            pltpu.VMEM((2, CHUNKS, NT, rows, HALF), BF16),
            pltpu.VMEM((2, CHUNKS, rows, COLS), F32),
            pltpu.VMEM((2, CHUNKS, rows, COLS), F32),
            pltpu.VMEM((3 * TALLY, 128), F32),
            dma(4),
            one, dma(CHUNKS), dma(CHUNKS), one, dma(CHUNKS),
            one, one, one, one,
            one, one, dma(2, CHUNKS),
            one, one, dma(2, CHUNKS),
            one, dma(2, CHUNKS),
            one, dma(3),
        ],
        compiler_params=pltpu.CompilerParams(
            collective_id=0, has_side_effects=True, vmem_limit_bytes=40 * 2**20
        ),
    )(*map(far_memory, (answer_len, queries, turn_kv, cache_kv, out_weight.T)))


def solution(mesh):
    return jax.shard_map(
        on_device,
        mesh=mesh,
        in_specs=(
            P(("prompt", "sample"), None, "tensor"),
            P(None, ("prompt", "sample"), None, "tensor"),
            P(None, ("prompt", "sample"), None, "tensor"),
            P("prompt"),
            P("tensor", "sample"),
        ),
        out_specs=P(("prompt", "tensor"), "sample"),
        check_vma=False,
    )
```
